32 devices in a mesh: dom: 2 (over y), feat: 4 (over z), tok: 4 (over x, core).
Axes of the slice: x: 2, y: 2, z: 4, core: 2. Of those that a mesh axis runs over, the one named last changes fastest.
Arguments:
- activations: bfloat16 [16384, 14336], P(('dom', 'tok'), 'feat'), parts along dimension 0, may hold values from -6 to 6
- out_grads: bfloat16 [16384, 4096], P(('dom', 'tok'), 'feat'), parts along dimension 0, may hold values from -6 to 6
- proj_in: bfloat16 [64, 14336], P(None, 'feat'), may hold values from -0.046875 to 0.046875
- proj_out: bfloat16 [64, 4096], P(None, 'feat'), may hold values from -0.09375 to 0.09375
- block_example: int32 [128], P(('dom', 'tok')), parts along dimension 0, may hold values from 0 to 31, as said below
- block_fill: int32 [128], P(('dom', 'tok')), parts along dimension 0, may hold values from 1 to 128
Outputs:
- features: float32 [64, 4096], P(('dom', 'tok'), 'feat'), parts along dimension 0
The draws below stay inside these ranges and needn't reach their ends.
There are 2 independent parts, one for each index of `dom`. The reference program is written for one: setup_inputs(seed, part) draws one part's arguments, and reference() takes and returns one part's arrays. A program takes and returns all parts, laid end to end along the dimension named above; an argument that names none is the same for every part. Nothing has to cross between parts.
Inputs may be any that keep to these rules, and one draw needn't show every extreme that they name: `block_example`: values are example numbers; example e's home is index e // 8 of tok. Among the blocks held by one index of tok, at most 8 belong to examples of any one home, and some home has exactly 8 of them in every draw.
All inputs are finite; a program needn't handle non-finite values.
Results may differ from the reference program's by a relative error of at most 0.0003.
Values sent between devices are 32-bit elements; how exact they have to be, the bound alone decides.
A program may use at most 64 MiB of HBM per device.

```python
import jax
import jax.numpy as jnp
from jax import lax

D = 4096
FF = 14336
R = 64
BLK = 128
TOK_DEV = 2048
EX_DEV = 8
TOKENS = 8192
BLOCKS = 64
EXAMPLES = 32


def draw_block_example(key, part):
    key = jax.random.fold_in(key, 7)
    homes = EXAMPLES // EX_DEV
    blocks_dev = TOK_DEV // BLK
    limit = max(2, 2 * ((blocks_dev + homes - 1) // homes))

    def one_source(source_key):
        key_home, key_pick, key_order, key_local = jax.random.split(source_key, 4)
        home_order = jax.random.permutation(key_home, homes).astype(jnp.int32)
        slot_home = jnp.repeat(home_order, limit)
        rest = jax.random.permutation(key_pick, homes * limit - limit)[:blocks_dev - limit] + limit
        picked = jnp.concatenate([jnp.arange(limit, dtype=jnp.int32), rest.astype(jnp.int32)])
        shuffled = jax.random.permutation(key_order, picked)
        local = jax.random.randint(key_local, (blocks_dev,), 0, EX_DEV, dtype=jnp.int32)
        return slot_home[shuffled] * EX_DEV + local
    source_keys = jax.random.split(key, homes)
    return jax.vmap(one_source)(source_keys).reshape(BLOCKS).astype(jnp.int32)


def plant(values, stream_key, low, largest):
    dims = values.shape
    place = [jax.random.randint(jax.random.fold_in(stream_key, axis), (), 0, dims[axis]) for axis in range(len(dims))]
    values = values.at[tuple(place)].set(low)
    longest = dims.index(max(dims))
    place[longest] = (place[longest] + 1) % dims[longest]
    return values.at[tuple(place)].set(largest)


def shard_levels(rng, shape, pieces, low, largest):
    loudness, own = 1.0, jax.random.fold_in(rng, 6)
    for dim, parts in pieces:
        draws = jnp.exp(jax.random.uniform(jax.random.fold_in(own, dim), (parts,), jnp.float32, low / len(pieces), largest / len(pieces)))
        loudness = loudness * jnp.repeat(draws, shape[dim] // parts).reshape([-1 if axis == dim else 1 for axis in range(len(shape))])
    return loudness


def normal_values(own_key, shape, spread, reach, pieces=(), kind=jnp.bfloat16):
    array = spread * jax.random.normal(own_key, shape, jnp.float32)
    if pieces:
        array = array * shard_levels(own_key, shape, pieces, -0.22, 0.18)
    return jnp.clip(array, -reach, reach).astype(kind)


def setup_inputs(seed: int = 0, part: int = 0) -> dict:
    streams_of = jax.random.split(jax.random.key(seed), 7)
    part_splits = jax.random.split(jax.random.fold_in(streams_of[6], part), 7)
    return {
        "activations": normal_values(part_splits[0], (TOKENS, FF), 1.0, 6.0, ((0, 4), (1, 4))),
        "out_grads": normal_values(part_splits[1], (TOKENS, D), 1.0, 6.0, ((0, 4), (1, 4))),
        "proj_in": normal_values(streams_of[2], (R, FF), FF ** -0.5, 0.046875, ((1, 4),)),
        "proj_out": normal_values(streams_of[3], (R, D), D ** -0.5, 0.09375, ((1, 4),)),
        "block_example": draw_block_example(jax.random.fold_in(jax.random.fold_in(streams_of[6], part), 71), part),
        "block_fill": plant(jax.random.randint(part_splits[5], (BLOCKS,), 1, BLK + 1), jax.random.fold_in(part_splits[5], 1), 1, BLK).astype(jnp.int32),
    }


feature_scale = 0.088388


def reference(activations, out_grads, proj_in, proj_out, block_example, block_fill):
    slots = jnp.arange(TOKENS, dtype=jnp.int32)
    block_of = (slots // BLK).astype(jnp.int32)
    live = ((slots % BLK) < block_fill[block_of]).astype(jnp.float32)
    example = block_example[block_of]
    side_in = jnp.dot(activations, proj_in.T, preferred_element_type=jnp.float32) * live[:, None]
    side_out = jnp.dot(out_grads, proj_out.T, preferred_element_type=jnp.float32) * live[:, None]

    def one_example(index):
        weight = (example == index).astype(jnp.float32)
        block = jnp.dot((side_out * weight[:, None]).T, side_in, precision=lax.Precision.HIGHEST, preferred_element_type=jnp.float32)
        return block.reshape(R * R)

    features = lax.map(one_example, jnp.arange(EXAMPLES, dtype=jnp.int32))
    return features * feature_scale
```

```python
import functools

import jax
import jax.numpy as jnp
from jax import lax
from jax.experimental import pallas as pl
from jax.experimental.pallas import tpu as pltpu
from jax.sharding import PartitionSpec as P

R = 64
BLK = 128
EX_DEV = 8
LANES = 128
NEAR_LAG = 2
FAR_LAG = 4
MESH = pl.DeviceIdType.MESH

feature_scale = 0.088388


def kernel(
    feats, toks, pieces,
    act_ref, grad_ref, pin_ref, pout_ref, example_ref, fill_ref,
    out_ref,
    act_buf, grad_buf, win, wout, own, inbox, square, gath, ids, acc, fin,
    load_sem, weight_sem, send_sem, recv_sem, block_send, block_recv,
    id_send, id_recv, fin_send, fin_recv,
):
    half = pieces * BLK
    f = lax.axis_index("feat")
    me = lax.axis_index("tok")
    part_rows = fin.shape[1]
    near = jnp.where(f < feats // 2, 0, 1)
    far = 1 - near
    is_end = jnp.logical_or(f == 0, f == feats - 1)
    is_mid = jnp.logical_not(is_end)

    def loads(p):
        copies = []
        for d in range(2):
            rows = pl.ds(pl.multiple_of((1 - d) * half + p * BLK, BLK), BLK)
            slot = pl.ds(d * BLK, BLK)
            copies.append(pltpu.make_async_copy(
                act_ref.at[rows], act_buf.at[p, slot], load_sem.at[p, 2 * d]))
            copies.append(pltpu.make_async_copy(
                grad_ref.at[rows], grad_buf.at[p, slot], load_sem.at[p, 2 * d + 1]))
        return copies

    win[...] = jnp.zeros_like(win)
    wout[...] = jnp.zeros_like(wout)
    weights = [
        pltpu.make_async_copy(pin_ref, win.at[pl.ds(R, R)], weight_sem.at[0]),
        pltpu.make_async_copy(pout_ref, wout.at[pl.ds(0, R)], weight_sem.at[1]),
    ]
    for copy in weights:
        copy.start()

    @pl.loop(0, pieces)
    def _(p):
        for copy in loads(p):
            copy.start()

    barrier = pltpu.get_barrier_semaphore()
    for j in range(1, feats):
        pl.semaphore_signal(
            barrier, inc=1, device_id={"feat": lax.rem(f + j, feats)}, device_id_type=MESH)
    for j in range(1, toks):
        pl.semaphore_signal(
            barrier, inc=1, device_id={"tok": lax.rem(me + j, toks)}, device_id_type=MESH)

    acc[...] = jnp.zeros_like(acc)
    for b in range(2 * pieces):
        ids[me, b] = jnp.full((LANES,), example_ref[b], jnp.int32).astype(jnp.float32)
    for copy in weights:
        copy.wait()
    pl.semaphore_wait(barrier, feats - 1 + toks - 1)

    def id_copy(j):
        return pltpu.make_async_remote_copy(
            src_ref=ids.at[me], dst_ref=ids.at[me],
            send_sem=id_send.at[j - 1], recv_sem=id_recv.at[me],
            device_id={"tok": lax.rem(me + j, toks)}, device_id_type=MESH)

    def id_arrival(t):
        return pltpu.make_async_remote_copy(
            src_ref=ids.at[me], dst_ref=ids.at[t],
            send_sem=id_send.at[0], recv_sem=id_recv.at[t],
            device_id={"tok": t}, device_id_type=MESH)

    def hop(d, p):
        return pltpu.make_async_remote_copy(
            src_ref=own.at[d, p], dst_ref=inbox.at[d, p],
            send_sem=send_sem.at[d, p], recv_sem=recv_sem.at[d, p],
            device_id={"feat": lax.rem(f + 1 - 2 * d + feats, feats)}, device_id_type=MESH)

    def block_copy(p, j):
        return pltpu.make_async_remote_copy(
            src_ref=gath.at[me, p], dst_ref=gath.at[me, p],
            send_sem=block_send.at[p, j - 1], recv_sem=block_recv.at[me, p],
            device_id={"tok": lax.rem(me + j, toks)}, device_id_type=MESH)

    def block_arrival(t, p):
        return pltpu.make_async_remote_copy(
            src_ref=gath.at[me, p], dst_ref=gath.at[t, p],
            send_sem=block_send.at[p, 0], recv_sem=block_recv.at[t, p],
            device_id={"tok": t}, device_id_type=MESH)

    @pl.when(is_end)
    def _():
        for j in range(1, toks):
            id_copy(j).start()

    contract = (((1,), (1,)), ((), ()))

    def project(p):
        for copy in loads(p):
            copy.wait()
        both = lax.dot_general(
            act_buf[p], win[...], contract, preferred_element_type=jnp.float32)
        both += lax.dot_general(
            grad_buf[p], wout[...], contract, preferred_element_type=jnp.float32)
        own[0, p] = both[:BLK]
        own[1, p] = both[BLK:]

    def forward(d, p):
        hop(d, p).wait_recv()
        own[d, p] += inbox[d, p]
        hop(d, p).start()

    @pl.loop(0, pieces + FAR_LAG)
    def _(step):
        @pl.when(step < pieces)
        def _():
            project(step)

            @pl.when(is_end)
            def _():
                hop(near, step).start()

        @pl.when(jnp.logical_and(is_mid, jnp.logical_and(step >= NEAR_LAG, step < pieces + NEAR_LAG)))
        def _():
            forward(near, step - NEAR_LAG)

        @pl.when(jnp.logical_and(is_mid, step >= FAR_LAG))
        def _():
            forward(far, step - FAR_LAG)

    lane = lax.broadcasted_iota(jnp.int32, (BLK, LANES), 1)
    row = lax.broadcasted_iota(jnp.int32, (BLK, LANES), 0)
    half_lane = lax.broadcasted_iota(jnp.int32, (R // 2, LANES), 1)
    home_example = (
        lax.broadcasted_iota(jnp.int32, (EX_DEV, LANES), 0) + me * EX_DEV
    ).astype(jnp.float32)

    def outer(p):
        hop(far, p).wait_recv()
        fill = fill_ref[p + (1 - far) * pieces]
        sides = jnp.where(row < fill, own[far, p] + inbox[far, p], 0.0)
        twice = jnp.where(lane < R, pltpu.roll(sides, R, 1), sides)
        square[...] = lax.dot_general(
            sides, twice, (((0,), (0,)), ((), ())),
            precision=lax.Precision.HIGHEST, preferred_element_type=jnp.float32)[:R]
        even = square[pl.ds(0, R // 2, stride=2), :]
        odd = square[pl.ds(1, R // 2, stride=2), :]
        gath[me, p] = jnp.where(half_lane < R, even, odd)
        for j in range(1, toks):
            block_copy(p, j).start()

    def gather(p):
        for j in range(toks):
            t = lax.rem(me + j, toks)
            if j:
                block_arrival(t, p).wait_recv()
            named = ids[t, pl.ds(p + (1 - far) * pieces, 1), :]
            member = jnp.where(home_example == named, 1.0, 0.0)
            acc[...] += gath[t, p][:, None, :] * member[None]

    def fin_copy(j):
        target = lax.rem(f + j, feats)
        return pltpu.make_async_remote_copy(
            src_ref=acc.at[pl.ds(target * part_rows, part_rows)], dst_ref=fin.at[far],
            send_sem=fin_send.at[j - 1], recv_sem=fin_recv.at[far],
            device_id={"feat": target}, device_id_type=MESH)

    def fin_arrival(slot):
        return pltpu.make_async_remote_copy(
            src_ref=acc.at[pl.ds(0, part_rows)], dst_ref=fin.at[slot],
            send_sem=fin_send.at[0], recv_sem=fin_recv.at[slot],
            device_id={"feat": lax.rem(f + 1, feats)}, device_id_type=MESH)

    @pl.when(is_end)
    def _():
        for j in range(1, toks):
            id_arrival(lax.rem(me + j, toks)).wait_recv()

        @pl.loop(0, pieces + 1)
        def _(p):
            @pl.when(p < pieces)
            def _():
                outer(p)

            @pl.when(p >= 1)
            def _():
                gather(p - 1)

        acc[...] = acc[...] * feature_scale
        for j in range(1, feats):
            fin_copy(j).start()
        fin[far] = acc[pl.ds(f * part_rows, part_rows)]
        fin_arrival(near).wait_recv()

    @pl.when(is_mid)
    def _():
        fin_arrival(0).wait_recv()
        fin_arrival(1).wait_recv()

    for r in range(part_rows):
        out_ref[:, r * LANES:(r + 1) * LANES] = fin[0, r] + fin[1, r]

    @pl.loop(0, pieces)
    def _(p):
        hop(near, p).wait_send()

        @pl.when(is_mid)
        def _():
            hop(far, p).wait_send()

        @pl.when(is_end)
        def _():
            for j in range(1, toks):
                block_copy(p, j).wait_send()

    @pl.when(is_end)
    def _():
        for j in range(1, toks):
            id_copy(j).wait_send()
        for j in range(1, feats):
            fin_copy(j).wait_send()


def shards(feats, toks, activations, out_grads, proj_in, proj_out, block_example, block_fill):
    rows, in_columns = activations.shape
    out_columns = out_grads.shape[1]
    pieces = rows // (2 * BLK)
    out_rows = R * R // LANES
    hbm = pl.BlockSpec(memory_space=pl.ANY)
    smem = pl.BlockSpec(memory_space=pltpu.SMEM)
    dma = pltpu.SemaphoreType.DMA
    return pl.pallas_call(
        functools.partial(kernel, feats, toks, pieces),
        out_shape=jax.ShapeDtypeStruct((EX_DEV, R * R // feats), jnp.float32),
        in_specs=[hbm, hbm, hbm, hbm, smem, smem],
        out_specs=pl.BlockSpec(memory_space=pltpu.VMEM),
        scratch_shapes=[
            pltpu.VMEM((pieces, 2 * BLK, in_columns), jnp.bfloat16),
            pltpu.VMEM((pieces, 2 * BLK, out_columns), jnp.bfloat16),
            pltpu.VMEM((LANES, in_columns), jnp.bfloat16),
            pltpu.VMEM((LANES, out_columns), jnp.bfloat16),
            pltpu.VMEM((2, pieces, BLK, LANES), jnp.float32),
            pltpu.VMEM((2, pieces, BLK, LANES), jnp.float32),
            pltpu.VMEM((R, LANES), jnp.float32),
            pltpu.VMEM((toks, pieces, out_rows, LANES), jnp.float32),
            pltpu.VMEM((toks, 2 * pieces, LANES), jnp.float32),
            pltpu.VMEM((out_rows, EX_DEV, LANES), jnp.float32),
            pltpu.VMEM((2, out_rows // feats, EX_DEV, LANES), jnp.float32),
            dma((pieces, 4)),
            dma((2,)),
            dma((2, pieces)),
            dma((2, pieces)),
            dma((pieces, toks - 1)),
            dma((toks, pieces)),
            dma((toks - 1,)),
            dma((toks,)),
            dma((feats - 1,)),
            dma((2,)),
        ],
        compiler_params=pltpu.CompilerParams(
            collective_id=0, has_side_effects=True, vmem_limit_bytes=48 * 2**20
        ),
        cost_estimate=pl.CostEstimate(
            flops=2 * rows * R * (in_columns + out_columns),
            bytes_accessed=2 * rows * (in_columns + out_columns),
            transcendentals=0,
        ),
    )(activations, out_grads, proj_in, proj_out, block_example, block_fill)


def solution(mesh):
    in_specs = (
        P(("dom", "tok"), "feat"),
        P(("dom", "tok"), "feat"),
        P(None, "feat"),
        P(None, "feat"),
        P(("dom", "tok")),
        P(("dom", "tok")),
    )
    out_specs = P(("dom", "tok"), "feat")
    body = functools.partial(shards, mesh.shape["feat"], mesh.shape["tok"])
    return jax.shard_map(body, mesh=mesh, in_specs=in_specs, out_specs=out_specs, check_vma=False)
```

```python
import functools

import jax
import jax.numpy as jnp
from jax import lax
from jax.experimental import pallas as pl
from jax.experimental.pallas import tpu as pltpu
from jax.sharding import PartitionSpec as P

R = 64
BLK = 128
EX_DEV = 8
LANES = 128
NEAR_LAG = 1
FAR_LAG = 4
MID_BLOCKS = 2
MESH = pl.DeviceIdType.MESH

feature_scale = 0.088388


def kernel(
    feats, toks, blocks, end_blocks, mid_blocks,
    act_ref, grad_ref, pin_ref, pout_ref, example_hbm, fill_hbm,
    out_ref,
    example_ref, fill_ref, act_buf, grad_buf, win, wout, own, inbox, square, gath, ids, acc, fin,
    load_sem, weight_sem, send_sem, recv_sem, block_send, block_recv,
    id_send, id_recv, fin_send, fin_recv,
):
    pieces = blocks // 2
    f = lax.axis_index("feat")
    me = lax.axis_index("tok")
    part_rows = fin.shape[1]
    near = jnp.where(f < feats // 2, 0, 1)
    far = 1 - near
    is_end = jnp.logical_or(f == 0, f == feats - 1)
    is_mid = jnp.logical_not(is_end)

    def first_block(owner):
        inner = end_blocks + (owner - 1) * mid_blocks
        return jnp.where(owner <= 0, 0, jnp.where(owner >= feats, blocks, inner))

    lower, upper = first_block(f), first_block(f + 1)
    owned = upper - lower
    rising = f < feats // 2
    near_count = jnp.where(rising, blocks - upper, lower)
    far_count = jnp.where(rising, lower, blocks - upper)

    def block_at(d, p):
        return d * p + (1 - d) * (blocks - 1 - p)

    def loads(p):
        copies = []
        for d in range(2):
            rows = pl.ds(pl.multiple_of(block_at(d, p) * BLK, BLK), BLK)
            slot = pl.ds(d * BLK, BLK)
            copies.append(pltpu.make_async_copy(
                act_ref.at[rows], act_buf.at[p, slot], load_sem.at[p, 2 * d]))
            copies.append(pltpu.make_async_copy(
                grad_ref.at[rows], grad_buf.at[p, slot], load_sem.at[p, 2 * d + 1]))
        return copies

    barrier = pltpu.get_barrier_semaphore()
    for j in range(1, feats):
        pl.semaphore_signal(
            barrier, inc=1, device_id={"feat": lax.rem(f + j, feats)}, device_id_type=MESH)
    for j in range(1, toks):
        pl.semaphore_signal(
            barrier, inc=1, device_id={"tok": lax.rem(me + j, toks)}, device_id_type=MESH)

    win[...] = jnp.zeros_like(win)
    wout[...] = jnp.zeros_like(wout)
    weights = [
        pltpu.make_async_copy(pin_ref, win.at[pl.ds(R, R)], weight_sem.at[0]),
        pltpu.make_async_copy(pout_ref, wout.at[pl.ds(0, R)], weight_sem.at[1]),
        pltpu.make_async_copy(example_hbm, example_ref, weight_sem.at[2]),
        pltpu.make_async_copy(fill_hbm, fill_ref, weight_sem.at[3]),
    ]
    for copy in weights:
        copy.start()

    @pl.loop(0, pieces)
    def _(p):
        for copy in loads(p):
            copy.start()

    for copy in weights:
        copy.wait()
    def id_copy(j):
        return pltpu.make_async_remote_copy(
            src_ref=ids.at[me], dst_ref=ids.at[me],
            send_sem=id_send.at[j - 1], recv_sem=id_recv.at[me],
            device_id={"tok": lax.rem(me + j, toks)}, device_id_type=MESH)

    def id_arrival(t):
        return pltpu.make_async_remote_copy(
            src_ref=ids.at[me], dst_ref=ids.at[t],
            send_sem=id_send.at[0], recv_sem=id_recv.at[t],
            device_id={"tok": t}, device_id_type=MESH)

    def hop(d, b):
        return pltpu.make_async_remote_copy(
            src_ref=own.at[b], dst_ref=inbox.at[d, b],
            send_sem=send_sem.at[b], recv_sem=recv_sem.at[d, b],
            device_id={"feat": lax.rem(f + 1 - 2 * d + feats, feats)}, device_id_type=MESH)

    def block_copy(p, j):
        return pltpu.make_async_remote_copy(
            src_ref=gath.at[me, p], dst_ref=gath.at[me, p],
            send_sem=block_send.at[p, j - 1], recv_sem=block_recv.at[me, p],
            device_id={"tok": lax.rem(me + j, toks)}, device_id_type=MESH)

    def block_arrival(t, p):
        return pltpu.make_async_remote_copy(
            src_ref=gath.at[me, p], dst_ref=gath.at[t, p],
            send_sem=block_send.at[p, 0], recv_sem=block_recv.at[t, p],
            device_id={"tok": t}, device_id_type=MESH)


    contract = (((1,), (1,)), ((), ()))

    def project(p):
        for copy in loads(p):
            copy.wait()
        both = lax.dot_general(
            act_buf[p], win[...], contract, preferred_element_type=jnp.float32)
        both += lax.dot_general(
            grad_buf[p], wout[...], contract, preferred_element_type=jnp.float32)
        own[block_at(0, p)] = both[:BLK]
        own[block_at(1, p)] = both[BLK:]

    def forward(d, q):
        b = block_at(d, q)
        hop(d, b).wait_recv()
        own[b] += inbox[d, b]
        hop(d, b).start()

    @pl.loop(0, blocks + FAR_LAG)
    def _(step):
        @pl.when(step < pieces)
        def _():
            project(step)

        @pl.when(step == 0)
        def _():
            pl.semaphore_wait(barrier, feats - 1 + toks - 1)

        @pl.when(jnp.logical_and(is_end, step < near_count))
        def _():
            hop(near, block_at(near, step)).start()

        @pl.when(jnp.logical_and(
            is_mid, jnp.logical_and(step >= NEAR_LAG, step < near_count + NEAR_LAG)))
        def _():
            forward(near, step - NEAR_LAG)

        @pl.when(jnp.logical_and(
            is_mid, jnp.logical_and(step >= FAR_LAG, step < far_count + FAR_LAG)))
        def _():
            forward(far, step - FAR_LAG)

    acc[...] = jnp.zeros_like(acc)
    for b in range(blocks):
        ids[me, b] = jnp.full((LANES,), example_ref[b], jnp.int32).astype(jnp.float32)
    for j in range(1, toks):
        id_copy(j).start()

    lane = lax.broadcasted_iota(jnp.int32, (BLK, LANES), 1)
    row = lax.broadcasted_iota(jnp.int32, (BLK, LANES), 0)
    half_lane = lax.broadcasted_iota(jnp.int32, (R // 2, LANES), 1)
    home_example = (
        lax.broadcasted_iota(jnp.int32, (EX_DEV, LANES), 0) + me * EX_DEV
    ).astype(jnp.float32)

    def block_of(i):
        return jnp.where(rising, lower + i, upper - 1 - i)

    def outer(i):
        b = block_of(i)

        @pl.when(f > 0)
        def _():
            hop(0, b).wait_recv()
            own[b] += inbox[0, b]

        @pl.when(f < feats - 1)
        def _():
            hop(1, b).wait_recv()
            own[b] += inbox[1, b]

        sides = jnp.where(row < fill_ref[b], own[b], 0.0)
        twice = jnp.where(lane < R, pltpu.roll(sides, R, 1), sides)
        square[...] = lax.dot_general(
            sides, twice, (((0,), (0,)), ((), ())),
            precision=lax.Precision.HIGHEST, preferred_element_type=jnp.float32)[:R]
        even = square[pl.ds(0, R // 2, stride=2), :]
        odd = square[pl.ds(1, R // 2, stride=2), :]
        gath[me, i] = jnp.where(half_lane < R, even, odd)
        for j in range(1, toks):
            block_copy(i, j).start()

    def gather(p):
        for j in range(toks):
            t = lax.rem(me + j, toks)
            if j:
                block_arrival(t, p).wait_recv()
            named = ids[t, pl.ds(block_of(p), 1), :]
            member = jnp.where(home_example == named, 1.0, 0.0)
            acc[...] += gath[t, p][:, None, :] * member[None]

    def fin_copy(j):
        target = lax.rem(f + j, feats)
        return pltpu.make_async_remote_copy(
            src_ref=acc.at[pl.ds(target * part_rows, part_rows)], dst_ref=fin.at[f],
            send_sem=fin_send.at[j - 1], recv_sem=fin_recv.at[f],
            device_id={"feat": target}, device_id_type=MESH)

    def fin_arrival(slot):
        return pltpu.make_async_remote_copy(
            src_ref=acc.at[pl.ds(0, part_rows)], dst_ref=fin.at[slot],
            send_sem=fin_send.at[0], recv_sem=fin_recv.at[slot],
            device_id={"feat": slot}, device_id_type=MESH)

    for j in range(1, toks):
        id_arrival(lax.rem(me + j, toks)).wait_recv()

    @pl.loop(0, owned)
    def _(i):
        outer(i)

    @pl.loop(0, owned)
    def _(i):
        gather(i)

    acc[...] = acc[...] * feature_scale
    for j in range(1, feats):
        fin_copy(j).start()
    fin[f] = acc[pl.ds(f * part_rows, part_rows)]
    for j in range(1, feats):
        fin_arrival(lax.rem(f + j, feats)).wait_recv()

    for r in range(part_rows):
        total = fin[0, r]
        for slot in range(1, feats):
            total += fin[slot, r]
        out_ref[:, r * LANES:(r + 1) * LANES] = total

    @pl.loop(0, near_count)
    def _(q):
        hop(near, block_at(near, q)).wait_send()

    @pl.loop(0, far_count)
    def _(q):
        hop(far, block_at(far, q)).wait_send()

    @pl.loop(0, owned)
    def _(i):
        for j in range(1, toks):
            block_copy(i, j).wait_send()

    for j in range(1, toks):
        id_copy(j).wait_send()
    for j in range(1, feats):
        fin_copy(j).wait_send()


def shards(feats, toks, activations, out_grads, proj_in, proj_out, block_example, block_fill):
    rows, in_columns = activations.shape
    out_columns = out_grads.shape[1]
    blocks = rows // BLK
    pieces = blocks // 2
    mid_blocks = max(0, min(MID_BLOCKS, (blocks - 2) // max(1, feats - 2)))
    end_blocks = (blocks - (feats - 2) * mid_blocks) // 2
    out_rows = R * R // LANES
    hbm = pl.BlockSpec(memory_space=pl.ANY)
    dma = pltpu.SemaphoreType.DMA
    return pl.pallas_call(
        functools.partial(kernel, feats, toks, blocks, end_blocks, mid_blocks),
        out_shape=jax.ShapeDtypeStruct((EX_DEV, R * R // feats), jnp.float32),
        in_specs=[hbm] * 6,
        out_specs=pl.BlockSpec(memory_space=pltpu.VMEM),
        scratch_shapes=[
            pltpu.SMEM(block_example.shape, jnp.int32),
            pltpu.SMEM(block_fill.shape, jnp.int32),
            pltpu.VMEM((pieces, 2 * BLK, in_columns), jnp.bfloat16),
            pltpu.VMEM((pieces, 2 * BLK, out_columns), jnp.bfloat16),
            pltpu.VMEM((LANES, in_columns), jnp.bfloat16),
            pltpu.VMEM((LANES, out_columns), jnp.bfloat16),
            pltpu.VMEM((blocks, BLK, LANES), jnp.float32),
            pltpu.VMEM((2, blocks, BLK, LANES), jnp.float32),
            pltpu.VMEM((R, LANES), jnp.float32),
            pltpu.VMEM((toks, blocks, out_rows, LANES), jnp.float32),
            pltpu.VMEM((toks, blocks, LANES), jnp.float32),
            pltpu.VMEM((out_rows, EX_DEV, LANES), jnp.float32),
            pltpu.VMEM((feats, out_rows // feats, EX_DEV, LANES), jnp.float32),
            dma((pieces, 4)),
            dma((4,)),
            dma((blocks,)),
            dma((2, blocks)),
            dma((blocks, toks - 1)),
            dma((toks, blocks)),
            dma((toks - 1,)),
            dma((toks,)),
            dma((feats - 1,)),
            dma((feats,)),
        ],
        compiler_params=pltpu.CompilerParams(
            collective_id=0, has_side_effects=True, vmem_limit_bytes=60 * 2**20
        ),
        cost_estimate=pl.CostEstimate(
            flops=2 * rows * R * (in_columns + out_columns),
            bytes_accessed=2 * rows * (in_columns + out_columns),
            transcendentals=0,
        ),
    )(activations, out_grads, proj_in, proj_out, block_example, block_fill)


def solution(mesh):
    in_specs = (
        P(("dom", "tok"), "feat"),
        P(("dom", "tok"), "feat"),
        P(None, "feat"),
        P(None, "feat"),
        P(("dom", "tok")),
        P(("dom", "tok")),
    )
    out_specs = P(("dom", "tok"), "feat")
    body = functools.partial(shards, mesh.shape["feat"], mesh.shape["tok"])
    return jax.shard_map(body, mesh=mesh, in_specs=in_specs, out_specs=out_specs, check_vma=False)
```

```python
import functools

import jax
import jax.numpy as jnp
from jax import lax
from jax.experimental import pallas as pl
from jax.experimental.pallas import tpu as pltpu
from jax.sharding import PartitionSpec as P

R = 64
BLK = 128
EX_DEV = 8
LANES = 128
NEAR_LAG = 1
FAR_LAG = 4
GATHER_LAG = 3
MID_BLOCKS = 2
MESH = pl.DeviceIdType.MESH

feature_scale = 0.088388


def kernel(
    feats, toks, blocks, end_blocks, mid_blocks,
    act_ref, grad_ref, pin_ref, pout_ref, example_hbm, fill_hbm,
    out_ref,
    example_ref, fill_ref, act_buf, grad_buf, win, wout, own, inbox, square, gath, ids, acc, fin,
    load_sem, weight_sem, send_sem, recv_sem, block_send, block_recv,
    id_send, id_recv, fin_send, fin_recv,
):
    pieces = blocks // 2
    f = lax.axis_index("feat")
    me = lax.axis_index("tok")
    part_rows = fin.shape[1]
    near = jnp.where(f < feats // 2, 0, 1)
    far = 1 - near
    is_end = jnp.logical_or(f == 0, f == feats - 1)
    is_mid = jnp.logical_not(is_end)

    def first_block(owner):
        inner = end_blocks + (owner - 1) * mid_blocks
        return jnp.where(owner <= 0, 0, jnp.where(owner >= feats, blocks, inner))

    lower, upper = first_block(f), first_block(f + 1)
    owned = upper - lower
    rising = f < feats // 2
    near_count = jnp.where(rising, blocks - upper, lower)
    far_count = jnp.where(rising, lower, blocks - upper)

    def block_at(d, p):
        return d * p + (1 - d) * (blocks - 1 - p)

    def loads(p):
        copies = []
        for d in range(2):
            rows = pl.ds(pl.multiple_of(block_at(d, p) * BLK, BLK), BLK)
            slot = pl.ds(d * BLK, BLK)
            copies.append(pltpu.make_async_copy(
                act_ref.at[rows], act_buf.at[p, slot], load_sem.at[p, 2 * d]))
            copies.append(pltpu.make_async_copy(
                grad_ref.at[rows], grad_buf.at[p, slot], load_sem.at[p, 2 * d + 1]))
        return copies

    barrier = pltpu.get_barrier_semaphore()
    for j in range(1, feats):
        pl.semaphore_signal(
            barrier, inc=1, device_id={"feat": lax.rem(f + j, feats)}, device_id_type=MESH)
    for j in range(1, toks):
        pl.semaphore_signal(
            barrier, inc=1, device_id={"tok": lax.rem(me + j, toks)}, device_id_type=MESH)

    win[...] = jnp.zeros_like(win)
    wout[...] = jnp.zeros_like(wout)
    weights = [
        pltpu.make_async_copy(pin_ref, win.at[pl.ds(R, R)], weight_sem.at[0]),
        pltpu.make_async_copy(pout_ref, wout.at[pl.ds(0, R)], weight_sem.at[1]),
        pltpu.make_async_copy(example_hbm, example_ref, weight_sem.at[2]),
        pltpu.make_async_copy(fill_hbm, fill_ref, weight_sem.at[3]),
    ]
    for copy in weights:
        copy.start()

    @pl.loop(0, pieces)
    def _(p):
        for copy in loads(p):
            copy.start()

    for copy in weights:
        copy.wait()
    def id_copy(j):
        return pltpu.make_async_remote_copy(
            src_ref=ids.at[me], dst_ref=ids.at[me],
            send_sem=id_send.at[j - 1], recv_sem=id_recv.at[me],
            device_id={"tok": lax.rem(me + j, toks)}, device_id_type=MESH)

    def id_arrival(t):
        return pltpu.make_async_remote_copy(
            src_ref=ids.at[me], dst_ref=ids.at[t],
            send_sem=id_send.at[0], recv_sem=id_recv.at[t],
            device_id={"tok": t}, device_id_type=MESH)

    def hop(d, b):
        return pltpu.make_async_remote_copy(
            src_ref=own.at[b], dst_ref=inbox.at[d, b],
            send_sem=send_sem.at[b], recv_sem=recv_sem.at[d, b],
            device_id={"feat": lax.rem(f + 1 - 2 * d + feats, feats)}, device_id_type=MESH)

    def block_copy(p, j):
        return pltpu.make_async_remote_copy(
            src_ref=gath.at[me, p], dst_ref=gath.at[me, p],
            send_sem=block_send.at[p, j - 1], recv_sem=block_recv.at[me, p],
            device_id={"tok": lax.rem(me + j, toks)}, device_id_type=MESH)

    def block_arrival(t, p):
        return pltpu.make_async_remote_copy(
            src_ref=gath.at[me, p], dst_ref=gath.at[t, p],
            send_sem=block_send.at[p, 0], recv_sem=block_recv.at[t, p],
            device_id={"tok": t}, device_id_type=MESH)


    contract = (((1,), (1,)), ((), ()))

    def project(p):
        for copy in loads(p):
            copy.wait()
        both = lax.dot_general(
            act_buf[p], win[...], contract, preferred_element_type=jnp.float32)
        both += lax.dot_general(
            grad_buf[p], wout[...], contract, preferred_element_type=jnp.float32)
        own[block_at(0, p)] = both[:BLK]
        own[block_at(1, p)] = both[BLK:]

    def forward(d, q):
        b = block_at(d, q)
        hop(d, b).wait_recv()
        own[b] += inbox[d, b]
        hop(d, b).start()

    @pl.loop(0, blocks + FAR_LAG)
    def _(step):
        @pl.when(step < pieces)
        def _():
            project(step)

        @pl.when(step == 0)
        def _():
            pl.semaphore_wait(barrier, feats - 1 + toks - 1)

        @pl.when(jnp.logical_and(is_end, step < near_count))
        def _():
            hop(near, block_at(near, step)).start()

        @pl.when(jnp.logical_and(
            is_mid, jnp.logical_and(step >= FAR_LAG, step < far_count + FAR_LAG)))
        def _():
            forward(far, step - FAR_LAG)

        @pl.when(jnp.logical_and(
            is_mid, jnp.logical_and(step >= NEAR_LAG, step < near_count + NEAR_LAG)))
        def _():
            forward(near, step - NEAR_LAG)

    acc[...] = jnp.zeros_like(acc)
    for b in range(blocks):
        ids[me, b] = jnp.full((LANES,), example_ref[b], jnp.int32).astype(jnp.float32)
    for j in range(1, toks):
        id_copy(j).start()

    lane = lax.broadcasted_iota(jnp.int32, (BLK, LANES), 1)
    row = lax.broadcasted_iota(jnp.int32, (BLK, LANES), 0)
    half_lane = lax.broadcasted_iota(jnp.int32, (R // 2, LANES), 1)
    home_example = (
        lax.broadcasted_iota(jnp.int32, (EX_DEV, LANES), 0) + me * EX_DEV
    ).astype(jnp.float32)

    def block_of(i):
        return jnp.where(rising, lower + i, upper - 1 - i)

    def outer(i):
        b = block_of(i)

        @pl.when(f > 0)
        def _():
            hop(0, b).wait_recv()
            own[b] += inbox[0, b]

        @pl.when(f < feats - 1)
        def _():
            hop(1, b).wait_recv()
            own[b] += inbox[1, b]

        sides = jnp.where(row < fill_ref[b], own[b], 0.0)
        twice = jnp.where(lane < R, pltpu.roll(sides, R, 1), sides)
        square[...] = lax.dot_general(
            sides, twice, (((0,), (0,)), ((), ())),
            precision=lax.Precision.HIGHEST, preferred_element_type=jnp.float32)[:R]
        even = square[pl.ds(0, R // 2, stride=2), :]
        odd = square[pl.ds(1, R // 2, stride=2), :]
        gath[me, i] = jnp.where(half_lane < R, even, odd)
        for j in range(1, toks):
            block_copy(i, j).start()

    def gather(p):
        for j in range(toks):
            t = lax.rem(me + j, toks)
            if j:
                block_arrival(t, p).wait_recv()
            named = ids[t, pl.ds(block_of(p), 1), :]
            member = jnp.where(home_example == named, 1.0, 0.0)
            acc[...] += gath[t, p][:, None, :] * member[None]

    def fin_copy(j):
        target = lax.rem(f + j, feats)
        return pltpu.make_async_remote_copy(
            src_ref=acc.at[pl.ds(target * part_rows, part_rows)], dst_ref=fin.at[f],
            send_sem=fin_send.at[j - 1], recv_sem=fin_recv.at[f],
            device_id={"feat": target}, device_id_type=MESH)

    def fin_arrival(slot):
        return pltpu.make_async_remote_copy(
            src_ref=acc.at[pl.ds(0, part_rows)], dst_ref=fin.at[slot],
            send_sem=fin_send.at[0], recv_sem=fin_recv.at[slot],
            device_id={"feat": slot}, device_id_type=MESH)

    for j in range(1, toks):
        id_arrival(lax.rem(me + j, toks)).wait_recv()

    @pl.loop(0, owned + GATHER_LAG)
    def _(i):
        @pl.when(i < owned)
        def _():
            outer(i)

        @pl.when(i >= GATHER_LAG)
        def _():
            gather(i - GATHER_LAG)

    acc[...] = acc[...] * feature_scale
    for j in range(1, feats):
        fin_copy(j).start()
    fin[f] = acc[pl.ds(f * part_rows, part_rows)]
    for j in range(1, feats):
        fin_arrival(lax.rem(f + j, feats)).wait_recv()

    for r in range(part_rows):
        total = fin[0, r]
        for slot in range(1, feats):
            total += fin[slot, r]
        out_ref[:, r * LANES:(r + 1) * LANES] = total

    @pl.loop(0, near_count)
    def _(q):
        hop(near, block_at(near, q)).wait_send()

    @pl.loop(0, far_count)
    def _(q):
        hop(far, block_at(far, q)).wait_send()

    @pl.loop(0, owned)
    def _(i):
        for j in range(1, toks):
            block_copy(i, j).wait_send()

    for j in range(1, toks):
        id_copy(j).wait_send()
    for j in range(1, feats):
        fin_copy(j).wait_send()


def shards(feats, toks, activations, out_grads, proj_in, proj_out, block_example, block_fill):
    rows, in_columns = activations.shape
    out_columns = out_grads.shape[1]
    blocks = rows // BLK
    pieces = blocks // 2
    mid_blocks = max(0, min(MID_BLOCKS, (blocks - 2) // max(1, feats - 2)))
    end_blocks = (blocks - (feats - 2) * mid_blocks) // 2
    out_rows = R * R // LANES
    hbm = pl.BlockSpec(memory_space=pl.ANY)
    dma = pltpu.SemaphoreType.DMA
    return pl.pallas_call(
        functools.partial(kernel, feats, toks, blocks, end_blocks, mid_blocks),
        out_shape=jax.ShapeDtypeStruct((EX_DEV, R * R // feats), jnp.float32),
        in_specs=[hbm] * 6,
        out_specs=pl.BlockSpec(memory_space=pltpu.VMEM),
        scratch_shapes=[
            pltpu.SMEM(block_example.shape, jnp.int32),
            pltpu.SMEM(block_fill.shape, jnp.int32),
            pltpu.VMEM((pieces, 2 * BLK, in_columns), jnp.bfloat16),
            pltpu.VMEM((pieces, 2 * BLK, out_columns), jnp.bfloat16),
            pltpu.VMEM((LANES, in_columns), jnp.bfloat16),
            pltpu.VMEM((LANES, out_columns), jnp.bfloat16),
            pltpu.VMEM((blocks, BLK, LANES), jnp.float32),
            pltpu.VMEM((2, blocks, BLK, LANES), jnp.float32),
            pltpu.VMEM((R, LANES), jnp.float32),
            pltpu.VMEM((toks, blocks, out_rows, LANES), jnp.float32),
            pltpu.VMEM((toks, blocks, LANES), jnp.float32),
            pltpu.VMEM((out_rows, EX_DEV, LANES), jnp.float32),
            pltpu.VMEM((feats, out_rows // feats, EX_DEV, LANES), jnp.float32),
            dma((pieces, 4)),
            dma((4,)),
            dma((blocks,)),
            dma((2, blocks)),
            dma((blocks, toks - 1)),
            dma((toks, blocks)),
            dma((toks - 1,)),
            dma((toks,)),
            dma((feats - 1,)),
            dma((feats,)),
        ],
        compiler_params=pltpu.CompilerParams(
            collective_id=0, has_side_effects=True, vmem_limit_bytes=60 * 2**20
        ),
        cost_estimate=pl.CostEstimate(
            flops=2 * rows * R * (in_columns + out_columns),
            bytes_accessed=2 * rows * (in_columns + out_columns),
            transcendentals=0,
        ),
    )(activations, out_grads, proj_in, proj_out, block_example, block_fill)


def solution(mesh):
    in_specs = (
        P(("dom", "tok"), "feat"),
        P(("dom", "tok"), "feat"),
        P(None, "feat"),
        P(None, "feat"),
        P(("dom", "tok")),
        P(("dom", "tok")),
    )
    out_specs = P(("dom", "tok"), "feat")
    body = functools.partial(shards, mesh.shape["feat"], mesh.shape["tok"])
    return jax.shard_map(body, mesh=mesh, in_specs=in_specs, out_specs=out_specs, check_vma=False)
```
